512 devices in a mesh: row: 64 (over z, y), col: 8 (over x, core).
Axes of the slice: x: 4, y: 4, z: 16, core: 2. Of those that a mesh axis runs over, the one named last changes fastest.
Arguments:
- acts: bfloat16 [8192, 8192], P('row'), may hold values from -22 to 22
- out_grads: bfloat16 [8192, 4096], P('row', 'col'), may hold values from -0.099436891 to 0.099436891
- weight: float32 [8192, 4096], P('row', 'col'), may hold values from -30 to 30
- row_state: float32 [8192], P('row'), may hold values from 0.002 to 2
- col_state: float32 [4096], P('col'), may hold values from 0.01 to 0.3
Outputs:
- new_weight: float32 [8192, 4096], P('row', 'col')
- update: float32 [8192, 4096], P('row', 'col')
- row_moment: float32 [8192], P('row')
- col_moment: float32 [4096], P('col')
The draws below stay inside these ranges and needn't reach their ends.
All inputs are finite; a program needn't handle non-finite values.
Results may differ from the reference program's by a relative error of at most 0.0003.
Values may be sent and summed in bfloat16 or wider, within the bound.
A program may use at most 64 MiB of HBM per device.

```python
import math
import jax
import jax.numpy as jnp
from jax import lax

D = 8192
HEAD_DIM = 256
HEADS = 16
FW = 4096
TOKENS = 8192


def row_ramp(count, top):
    frac = jnp.arange(count, dtype=jnp.float32) / jnp.float32(max(count - 1, 1))
    return jnp.exp(jnp.log(jnp.float32(top)) * frac)


def group_factor(count):
    tok_first = (jnp.arange(TOKENS) < TOKENS // 2)[:, None]
    feat_first = (jnp.arange(count) < count // 2)[None, :]
    return jnp.where(jnp.logical_and(tok_first, feat_first), 1.5, 0.5).astype(jnp.float32)


def draw_acts(key, part):
    inner = jax.random.fold_in(key, 11)
    values = jnp.clip(jax.random.normal(inner, (TOKENS, D), jnp.float32), -6.0, 6.0)
    values = values * jnp.sqrt(row_ramp(D, 30.0))[None, :]
    values = values * group_factor(D)
    return values.astype(jnp.bfloat16)


def draw_out_grads(key, part):
    inner = jax.random.fold_in(key, 23)
    scale = 1.0 / jnp.sqrt(jnp.float32(TOKENS))
    values = jnp.clip(jax.random.normal(inner, (TOKENS, FW), jnp.float32), -6.0, 6.0)
    values = values * group_factor(FW)
    return (values * scale).astype(jnp.bfloat16)


def column_factor(key):
    head_key = jax.random.fold_in(key, 53)
    head_scale = jnp.exp(jax.random.uniform(head_key, (HEADS,), jnp.float32, -1.2, 0.0))
    per_column = jnp.repeat(head_scale, HEAD_DIM)
    frac = jnp.arange(FW, dtype=jnp.float32) / jnp.float32(max(FW - 1, 1))
    return per_column * jnp.exp(-0.8 * frac)


def draw_weight(key, part):
    inner = jax.random.fold_in(key, 37)
    values = jnp.clip(jax.random.normal(inner, (D, FW), jnp.float32), -3.0, 3.0)
    values = values * row_ramp(D, 10.0)[:, None]
    return values * column_factor(key)[None, :]


def draw_row_state(key, part):
    inner = jax.random.fold_in(key, 41)
    noise = jnp.exp(jax.random.uniform(inner, (D,), jnp.float32, -0.6931472, 0.6931472))
    values = 0.5 * row_ramp(D, 0.02) * noise
    return values


def steps_of(stream_key, dims, cuts, least, high):
    level = 1.0
    for axis_at, shards_of in cuts:
        draws = jax.random.uniform(jax.random.fold_in(jax.random.fold_in(stream_key, 6), axis_at), (shards_of,), jnp.float32, least / len(cuts), high / len(cuts))
        level = level * jnp.repeat(jnp.exp(draws), dims[axis_at] // shards_of).reshape((-1,) + (1,) * (len(dims) - 1 - axis_at))
    return level


def setup_inputs(seed: int = 0) -> dict:
    splits = jax.random.split(jax.random.key(seed), 6)
    return {
        "acts": draw_acts(jax.random.fold_in(splits[5], 71), 0),
        "out_grads": draw_out_grads(jax.random.fold_in(splits[5], 71), 0),
        "weight": draw_weight(jax.random.fold_in(splits[5], 71), 0),
        "row_state": draw_row_state(jax.random.fold_in(splits[5], 71), 0),
        "col_state": jnp.clip(jnp.exp(math.log(0.3) - 3.4011974 * jax.random.uniform(splits[4], (FW,), jnp.float32) ** steps_of(splits[4], (FW,), ((0, 8),), -0.2, 0.2)), 0.01, 0.3),
    }


decay_rate = 0.85
floor_eps = 1e-30
relative_rate = 0.05

def reference(acts, out_grads, weight, row_state, col_state):
    gradient = lax.dot_general(acts, out_grads, (((0,), (0,)), ((), ())), preferred_element_type=jnp.float32)
    squares = gradient * gradient + floor_eps
    row_moment = decay_rate * row_state + (1.0 - decay_rate) * lax.optimization_barrier(jnp.mean(squares, axis=1))
    col_moment = decay_rate * col_state + (1.0 - decay_rate) * lax.optimization_barrier(jnp.mean(squares, axis=0))
    unclipped = gradient * lax.rsqrt(row_moment[:, None] * col_moment[None, :])
    clip_factor = jnp.maximum(1.0, jnp.sqrt(jnp.mean(unclipped * unclipped)))
    update = unclipped / clip_factor
    step_size = relative_rate * jnp.sqrt(jnp.mean(weight * weight) + 1e-06)
    new_weight = weight - step_size * update
    return (new_weight, update, row_moment, col_moment)
```

```python
import jax
import jax.numpy as jnp
from jax import lax
from jax.sharding import Mesh
from jax.sharding import PartitionSpec as P

Z, Y = "row_0", "row_1"
ROW = (Z, Y)
COL = ("col_0", "col_1")

decay_rate = 0.85
floor_eps = 1e-30
relative_rate = 0.05


def per_device(acts, out_grads, weight, row_state, col_state):
    n_row = lax.axis_size(ROW)
    n_z = lax.axis_size(Z)
    n_y = lax.axis_size(Y)
    n_col = lax.axis_size(COL)
    tok_dev = acts.shape[0]
    width = acts.shape[1]
    cols_here = out_grads.shape[1]
    cols_all = cols_here * n_col
    share_rows = tok_dev // n_col
    own_rows = lax.dynamic_slice_in_dim(acts, lax.axis_index(COL) * share_rows, share_rows, 0)
    arrived = lax.all_to_all(own_rows, Z, split_axis=1, concat_axis=0, tiled=True)
    columns = lax.all_gather(arrived.reshape(n_z, share_rows, width // n_z), COL, axis=1, tiled=True)
    columns = columns.reshape(n_z * tok_dev, width // n_z)
    gathered = lax.all_gather(out_grads, Z, axis=0, tiled=True)
    partial = lax.dot_general(
        columns, gathered, (((0,), (0,)), ((), ())), preferred_element_type=jnp.float32
    )
    gradient = lax.psum_scatter(partial, Y, scatter_dimension=0, tiled=True)
    squares = gradient * gradient + floor_eps
    row_squares = jnp.sum(squares, axis=1)
    col_squares = jnp.sum(squares, axis=0)
    weight_part = jnp.sum(weight * weight)
    row_total = lax.psum(row_squares, COL)
    row_moment = decay_rate * row_state + (1.0 - decay_rate) * (row_total / cols_all)
    scaled = gradient * lax.rsqrt(row_moment)[:, None]
    stacked = jnp.concatenate([col_squares, jnp.sum(scaled * scaled, axis=0)])
    stacked = lax.psum(stacked, ROW)
    col_total, scaled_total = stacked[:cols_here], stacked[cols_here:]
    col_moment = decay_rate * col_state + (1.0 - decay_rate) * (col_total / width)
    unclipped = gradient * lax.rsqrt(row_moment[:, None] * col_moment[None, :])
    update_total = lax.psum(jnp.sum(scaled_total / col_moment), COL)
    weight_total = lax.psum(weight_part, ROW + COL)
    count_all = width * cols_all
    clip_factor = jnp.maximum(1.0, jnp.sqrt(update_total / count_all))
    update = unclipped / clip_factor
    step_size = relative_rate * jnp.sqrt(weight_total / count_all + 1e-06)
    new_weight = weight - step_size * update
    return (new_weight, update, row_moment, col_moment)


def solution(mesh):
    finer = Mesh(mesh.devices.reshape(16, 4, 4, 2), (Z, Y) + COL)
    placed = (P(ROW, None), P(ROW, COL), P(ROW, COL), P(ROW), P(COL))
    return jax.shard_map(
        per_device,
        mesh=finer,
        in_specs=placed,
        out_specs=(P(ROW, COL), P(ROW, COL), P(ROW), P(COL)),
        check_vma=False,
    )
```

```python
import functools

import jax
import jax.numpy as jnp
from jax import lax
from jax.experimental import pallas as pl
from jax.experimental.pallas import tpu as pltpu
from jax.sharding import Mesh
from jax.sharding import PartitionSpec as P

Z, Y, X, C = "z", "y", "x", "c"
ROW = (Z, Y)
COL = (X, C)
LANE = 128

decay_rate = 0.85
floor_eps = 1e-30
relative_rate = 0.05


def kernel(
    sizes,
    acts, og, weight, row_state, col_state,
    grad_out, row_out, col_out, scal_out,
    A, G, part, R, wv, rs_v, cs_v, st1, st2, st3, st4,
    local_sem, a2a_send, a2a_recv, x_send, x_recv, d_send, d_recv,
    ring_send, ring_recv, y_send, y_recv, st_send, st_recv,
):
    nz, ny, nx, nc, tok, cols, width = sizes
    half = nz // 2
    groups = cols // LANE
    rows_z = ny * LANE
    share = tok // (nx * nc)
    core_rows = share * nx
    cols_all = cols * nx * nc
    z, y, x, c = (lax.axis_index(a) for a in (Z, Y, X, C))
    xc = x * nc + c
    own = c * core_rows + x * share

    def to_z(d):
        return lax.rem(z + d, nz)

    def remote(src, dst, send, recv, where):
        return pltpu.make_async_remote_copy(
            src_ref=src, dst_ref=dst, send_sem=send, recv_sem=recv,
            device_id=where, device_id_type=pl.DeviceIdType.MESH,
        )

    def wait_bytes(ref, sem):
        pltpu.make_async_copy(ref, ref, sem).wait()

    def col_peer(k):
        i = lax.rem(xc + k, nx * nc)
        return {X: i // nc, C: lax.rem(i, nc)}

    barrier = pltpu.get_barrier_semaphore()
    for d in range(1, nz):
        pl.semaphore_signal(barrier, inc=1, device_id={Z: to_z(d)}, device_id_type=pl.DeviceIdType.MESH)
    for d in range(1, ny):
        pl.semaphore_signal(barrier, inc=1, device_id={Y: lax.rem(y + d, ny)}, device_id_type=pl.DeviceIdType.MESH)
    for k in range(1, nx * nc):
        pl.semaphore_signal(barrier, inc=1, device_id=col_peer(k), device_id_type=pl.DeviceIdType.MESH)

    own_cols = pl.ds(pl.multiple_of(z * rows_z, LANE), rows_z)
    local = [
        pltpu.make_async_copy(acts.at[:, own_cols], A.at[0, 0], local_sem.at[0]),
        pltpu.make_async_copy(og, G.at[0, 0], local_sem.at[1]),
        pltpu.make_async_copy(weight, wv, local_sem.at[2]),
        pltpu.make_async_copy(row_state, rs_v, local_sem.at[3]),
        pltpu.make_async_copy(col_state, cs_v, local_sem.at[4]),
    ]
    for copy in local:
        copy.start()
    part[...] = jnp.zeros_like(part)
    pl.semaphore_wait(barrier, nz - 1 + ny - 1 + nx * nc - 1)

    own_rows = pl.ds(pl.multiple_of(own, share), share)

    def send_acts(target, p, q, send, recv):
        there = pl.ds(pl.multiple_of(target * rows_z, LANE), rows_z)
        remote(acts.at[own_rows, there], A.at[p, q, own_rows, :], send, recv, {Z: target}).start()

    def send_pair(h, carry):
        send_acts(to_z(h), h, 0, a2a_send.at[0], a2a_recv.at[h])
        send_acts(to_z(nz - h), h, 1, a2a_send.at[0], a2a_recv.at[h])
        return carry

    lax.fori_loop(1, half, send_pair, 0)
    send_acts(to_z(half), 0, 1, a2a_send.at[1], a2a_recv.at[0])

    for copy in local:
        copy.wait()

    def last_hop(way, g):
        return half if (g < groups // 2) == (way == 0) else half - 1

    def ring_sem(way, g):
        return ring_send.at[way, 0 if last_hop(way, g) == half else 1]

    def lanes(g):
        return pl.ds(g * LANE, LANE)

    def ring_copy(way, g, h):
        src = G.at[h, way, :, lanes(g)] if not isinstance(h, int) else G.at[0, 0, :, lanes(g)]
        nxt = h + 1
        q = nxt // half if way == 0 else 1
        return remote(
            src, G.at[lax.rem(nxt, half), q, :, lanes(g)], ring_sem(way, g), ring_recv.at[way, g, h],
            {Z: to_z(1 if way == 0 else nz - 1)},
        )

    def x_pair(p):
        for d in range(1, nx):
            there = {X: lax.rem(x + d, nx)}
            mine = A.at[p, :, own_rows, :]
            remote(mine, mine, x_send.at[0], x_recv.at[p], there).start()

    def x_last():
        for d in range(1, nx):
            there = {X: lax.rem(x + d, nx)}
            mine = A.at[0, 1, own_rows, :]
            remote(mine, mine, x_send.at[1], x_recv.at[0], there).start()

    core_part = pl.ds(pl.multiple_of(c * core_rows, core_rows), core_rows)
    sibling = {C: nc - 1 - c}

    def step(s, carry):
        for g in range(groups):
            @pl.when(s == g + 1)
            def _():
                for way in range(2):
                    ring_copy(way, g, 0).start()

        r = s - 2
        for g in range(groups):
            h = r - g
            for way in range(2):
                last = last_hop(way, g)

                @pl.when(jnp.logical_and(h >= 1, h <= last))
                def _():
                    wait_bytes(G.at[0, 0, :, lanes(g)], ring_recv.at[way, g, h - 1])

                @pl.when(jnp.logical_and(h >= 1, h < last))
                def _():
                    ring_copy(way, g, h).start()

        @pl.when(s < half)
        def _():
            wait_bytes(A.at[0, :, pl.ds(0, share), :], a2a_recv.at[s])
            x_pair(s)

        @pl.when(s == half)
        def _():
            wait_bytes(A.at[0, 0, pl.ds(0, share), :], a2a_recv.at[0])
            x_last()

        @pl.when(jnp.logical_and(s >= 2, s <= half))
        def _():
            wait_bytes(A.at[0, :, pl.ds(0, share * (nx - 1)), :], x_recv.at[s - 1])
            mine = A.at[s - 1, :, core_part, :]
            remote(mine, mine, d_send.at[0], d_recv.at[s - 1], sibling).start()

        @pl.when(s == half + 1)
        def _():
            wait_bytes(A.at[0, 0, pl.ds(0, share * (nx - 1)), :], x_recv.at[0])
            mine = A.at[0, 1, core_part, :]
            remote(mine, mine, d_send.at[1], d_recv.at[0], sibling).start()

        @pl.when(jnp.logical_and(s >= 3, s <= half + 1))
        def _():
            wait_bytes(A.at[0, :, pl.ds(0, core_rows), :], d_recv.at[s - 2])

        @pl.when(s == half + 2)
        def _():
            wait_bytes(A.at[0, 0, pl.ds(0, core_rows), :], d_recv.at[0])

        for g in range(groups):
            h = r - g

            @pl.when(jnp.logical_and(h >= 1, h <= half))
            def _():
                p = lax.rem(h, half)
                grads = G[p, :, :, g * LANE:(g + 1) * LANE].reshape(2 * tok, LANE)
                block = A[p].reshape(2 * tok, rows_z)
                product = lax.dot_general(
                    grads, block, (((0,), (0,)), ((), ())), preferred_element_type=jnp.float32
                )
                for yy in range(ny):
                    part[g, yy] += product[:, yy * LANE:(yy + 1) * LANE]

            @pl.when(h == half)
            def _():
                for d in range(1, ny):
                    there = lax.rem(y + d, ny)
                    remote(part.at[g, there], R.at[g, d - 1], y_send.at[0], y_recv.at[g], {Y: there}).start()

        return carry

    lax.fori_loop(1, half + groups + 2, step, 0)

    weight_sq = jnp.sum(wv[...] * wv[...], axis=0, keepdims=True)
    weight_sq = sum(weight_sq[:, g * LANE:(g + 1) * LANE] for g in range(groups))

    row_sq = jnp.zeros((1, LANE), jnp.float32)
    for g in range(groups):
        wait_bytes(R.at[0], y_recv.at[g])
        total = part[g, y]
        for d in range(ny - 1):
            total += R[g, d]
        row_sq += jnp.sum(total * total + floor_eps, axis=0, keepdims=True)
        grad_out[:, g * LANE:(g + 1) * LANE] = total.T

    st1[xc] = jnp.broadcast_to(row_sq, (8, LANE))
    for k in range(1, nx * nc):
        remote(st1.at[xc], st1.at[xc], st_send.at[0], st_recv.at[0], col_peer(k)).start()
    for g in range(groups):
        grads = grad_out[:, g * LANE:(g + 1) * LANE]
        st2[y, g:g + 1, :] = jnp.sum(grads * grads + floor_eps, axis=0, keepdims=True)
    st2[y, 8:16, :] = jnp.broadcast_to(weight_sq, (8, LANE))
    wait_bytes(A.at[pl.ds(0, half - 1), :, pl.ds(0, share), :], a2a_send.at[0])
    wait_bytes(A.at[0, 0, pl.ds(0, share), :], a2a_send.at[1])
    wait_bytes(A.at[pl.ds(0, half - 1), :, pl.ds(0, share * (nx - 1)), :], x_send.at[0])
    wait_bytes(A.at[0, 0, pl.ds(0, share * (nx - 1)), :], x_send.at[1])
    wait_bytes(A.at[pl.ds(0, half - 1), :, pl.ds(0, core_rows), :], d_send.at[0])
    wait_bytes(A.at[0, 0, pl.ds(0, core_rows), :], d_send.at[1])
    for way in range(2):
        wait_bytes(G.at[:, 0, :, pl.ds(0, cols // 2)], ring_send.at[way, 0])
        wait_bytes(G.at[pl.ds(0, half - 1), 0, :, pl.ds(0, cols // 2)], ring_send.at[way, 1])
    wait_bytes(part.at[:, pl.ds(0, ny - 1)], y_send.at[0])

    wait_bytes(st1.at[pl.ds(0, nx * nc - 1)], st_recv.at[0])
    row_total = st1[0, 0:1, :]
    for k in range(1, nx * nc):
        row_total += st1[k, 0:1, :]
    row_moment = decay_rate * rs_v[...] + (1.0 - decay_rate) * (row_total / cols_all)
    row_out[...] = row_moment
    inverse = jnp.broadcast_to(1.0 / row_moment, (LANE, LANE)).T
    for g in range(groups):
        grads = grad_out[:, g * LANE:(g + 1) * LANE]
        st2[y, 4 + g:5 + g, :] = jnp.sum(grads * grads * inverse, axis=0, keepdims=True)

    for d in range(1, ny):
        remote(st2.at[y], st2.at[y], st_send.at[1], st_recv.at[1], {Y: lax.rem(y + d, ny)}).start()
    wait_bytes(st1.at[pl.ds(0, nx * nc - 1)], st_send.at[0])
    wait_bytes(st2.at[pl.ds(0, ny - 1)], st_recv.at[1])
    over_y = st2[0]
    for d in range(1, ny):
        over_y += st2[d]
    st3[z] = over_y
    for d in range(1, nz):
        remote(st3.at[z], st3.at[z], st_send.at[2], st_recv.at[2], {Z: to_z(d)}).start()
    wait_bytes(st2.at[pl.ds(0, ny - 1)], st_send.at[1])
    wait_bytes(st3.at[pl.ds(0, nz - 1)], st_recv.at[2])
    over_z = st3[0]
    for d in range(1, nz):
        over_z += st3[d]
    col_moment = decay_rate * cs_v[...] + (1.0 - decay_rate) * (over_z[0:groups] / width)
    col_out[...] = col_moment
    st4[xc, 0:4, :] = over_z[4:4 + groups] / col_moment
    st4[xc, 4:8, :] = over_z[8:12]

    for k in range(1, nx * nc):
        remote(st4.at[xc], st4.at[xc], st_send.at[3], st_recv.at[3], col_peer(k)).start()
    wait_bytes(st3.at[pl.ds(0, nz - 1)], st_send.at[2])
    wait_bytes(st4.at[pl.ds(0, nx * nc - 1)], st_recv.at[3])
    over_x = st4[0]
    for k in range(1, nx * nc):
        over_x += st4[k]
    scal_out[0:1, :] = jnp.broadcast_to(jnp.sum(over_x[0:4], keepdims=True), (1, LANE))
    scal_out[1:2, :] = jnp.broadcast_to(jnp.sum(over_x[4:5], keepdims=True), (1, LANE))
    wait_bytes(st4.at[pl.ds(0, nx * nc - 1)], st_send.at[3])


def per_device(acts, out_grads, weight, row_state, col_state):
    nz, ny, nx, nc = (lax.axis_size(a) for a in (Z, Y, X, C))
    tok, width = acts.shape
    cols = out_grads.shape[1]
    groups = cols // LANE
    half = nz // 2
    rows_z = ny * LANE
    anywhere = pl.BlockSpec(memory_space=pl.ANY)
    vmem = pl.BlockSpec(memory_space=pltpu.VMEM)
    f32 = jnp.float32
    gradient, row_moment, col_moment, scalars = pl.pallas_call(
        functools.partial(kernel, (nz, ny, nx, nc, tok, cols, width)),
        out_shape=(
            jax.ShapeDtypeStruct((LANE, cols), f32),
            jax.ShapeDtypeStruct((1, LANE), f32),
            jax.ShapeDtypeStruct((groups, LANE), f32),
            jax.ShapeDtypeStruct((8, LANE), f32),
        ),
        in_specs=[anywhere] * 5,
        out_specs=[vmem] * 4,
        scratch_shapes=[
            pltpu.VMEM((half, 2, tok, rows_z), jnp.bfloat16),
            pltpu.VMEM((half, 2, tok, cols), jnp.bfloat16),
            pltpu.VMEM((groups, ny, LANE, LANE), f32),
            pltpu.VMEM((groups, ny - 1, LANE, LANE), f32),
            pltpu.VMEM((LANE, cols), f32),
            pltpu.VMEM((1, LANE), f32),
            pltpu.VMEM((groups, LANE), f32),
            pltpu.VMEM((nx * nc, 8, LANE), f32),
            pltpu.VMEM((ny, 16, LANE), f32),
            pltpu.VMEM((nz, 16, LANE), f32),
            pltpu.VMEM((nx * nc, 8, LANE), f32),
            pltpu.SemaphoreType.DMA((5,)),
            pltpu.SemaphoreType.DMA((2,)),
            pltpu.SemaphoreType.DMA((half,)),
            pltpu.SemaphoreType.DMA((2,)),
            pltpu.SemaphoreType.DMA((half,)),
            pltpu.SemaphoreType.DMA((2,)),
            pltpu.SemaphoreType.DMA((half,)),
            pltpu.SemaphoreType.DMA((2, 2)),
            pltpu.SemaphoreType.DMA((2, groups, half)),
            pltpu.SemaphoreType.DMA((1,)),
            pltpu.SemaphoreType.DMA((groups,)),
            pltpu.SemaphoreType.DMA((4,)),
            pltpu.SemaphoreType.DMA((4,)),
        ],
        compiler_params=pltpu.CompilerParams(
            collective_id=0, has_side_effects=True, vmem_limit_bytes=32 * 1024 * 1024
        ),
    )(acts, out_grads, weight, row_state.reshape(1, LANE), col_state.reshape(groups, LANE))
    count_all = width * cols * nx * nc
    row_moment = row_moment.reshape(-1)
    col_moment = col_moment.reshape(-1)
    clip_factor = jnp.maximum(1.0, jnp.sqrt(scalars[0, 0] / count_all))
    step_size = relative_rate * jnp.sqrt(scalars[1, 0] / count_all + 1e-06)
    unclipped = gradient * lax.rsqrt(row_moment[:, None] * col_moment[None, :])
    update = unclipped / clip_factor
    new_weight = weight - step_size * update
    return (new_weight, update, row_moment, col_moment)


def solution(mesh):
    finer = Mesh(mesh.devices.reshape(16, 4, 4, 2), (Z, Y, X, C))
    return jax.shard_map(
        per_device,
        mesh=finer,
        in_specs=(P(ROW, None), P(ROW, COL), P(ROW, COL), P(ROW), P(COL)),
        out_specs=(P(ROW, COL), P(ROW, COL), P(ROW), P(COL)),
        check_vma=False,
    )
```

```python
import functools

import jax
import jax.numpy as jnp
from jax import lax
from jax.experimental import pallas as pl
from jax.experimental.pallas import tpu as pltpu
from jax.sharding import Mesh
from jax.sharding import PartitionSpec as P

Z, Y, X, C = "z", "y", "x", "c"
ROW = (Z, Y)
COL = (X, C)
LANE = 128
LAG = (0, 0, 1, 1)
BATCHES = (([0, 1], 2), ([2, 3], 3), ([4, 5], 4), ([6], 5), ([7], 5))

decay_rate = 0.85
floor_eps = 1e-30
relative_rate = 0.05


def plan(half, groups, lag, batches):
    steps = [("first", g) for g in range(groups) if lag[g] == 0]
    steps.append(("acts",))
    steps += [("first", g) for g in range(groups) if lag[g] == 1]
    ready, done = [], {g: [] for g in range(groups)}
    arrived = {g: [] for g in range(groups)}
    for r in range(1, half + max(lag) + 1):
        for g in range(groups):
            if lag[g] == r and r > 1:
                steps.append(("first", g))
            h = r - lag[g]
            if 1 <= h <= half:
                steps.append(("hop", g, h))
                arrived[g].append(h - 1)
        for stage in (1, 2, 3):
            for pairs, at in batches:
                if at + stage - 1 == r:
                    steps.append(("pairs", stage, pairs))
                    if stage == 3:
                        ready += pairs
        for g in range(groups):
            todo = [i for i in arrived[g] if i in ready and i not in done[g]]
            done[g] += todo
            if todo:
                steps.append(("dot", g, todo))
            if r - lag[g] == half:
                assert len(done[g]) == half
                steps.append(("scatter", g))
    return steps


def kernel(
    sizes,
    acts, og, weight, row_state, col_state,
    unclipped_out, row_out, col_out, clip_out, step_out,
    A, G, part, R, grad, wv, rs_v, cs_v, st1, st2, st3, st4,
    local_sem, a2a_send, a2a_recv, x_send, x_recv, d_send, d_recv,
    ring_send, ring_recv, y_send, y_recv, st_send, st_recv,
):
    nz, ny, nx, nc, tok, cols, width = sizes
    half = nz // 2
    groups = cols // LANE
    rows_z = ny * LANE
    share = tok // (nx * nc)
    core_rows = share * nx
    cols_all = cols * nx * nc
    count_all = width * cols_all
    z, y, x, c = (lax.axis_index(a) for a in (Z, Y, X, C))
    xc = x * nc + c
    own = c * core_rows + x * share
    far = half - 1

    def to_z(d):
        return lax.rem(z + d, nz)

    def remote(src, dst, send, recv, where):
        return pltpu.make_async_remote_copy(
            src_ref=src, dst_ref=dst, send_sem=send, recv_sem=recv,
            device_id=where, device_id_type=pl.DeviceIdType.MESH,
        )

    def wait_bytes(ref, sem):
        pltpu.make_async_copy(ref, ref, sem).wait()

    def col_peer(k):
        i = lax.rem(xc + k, nx * nc)
        return {X: i // nc, C: lax.rem(i, nc)}

    own_cols = pl.ds(pl.multiple_of(z * rows_z, LANE), rows_z)
    local = [
        pltpu.make_async_copy(og.at[:, pl.ds(g * LANE, LANE)], G.at[g, far, 0], local_sem.at[g])
        for g in range(groups)
    ] + [
        pltpu.make_async_copy(acts.at[:, own_cols], A.at[far, 0], local_sem.at[groups]),
        pltpu.make_async_copy(weight, wv, local_sem.at[groups + 1]),
        pltpu.make_async_copy(row_state, rs_v, local_sem.at[groups + 2]),
        pltpu.make_async_copy(col_state, cs_v, local_sem.at[groups + 3]),
    ]

    barrier = pltpu.get_barrier_semaphore()
    for d in sorted(range(1, nz), key=lambda d: -min(d, nz - d)):
        pl.semaphore_signal(barrier, inc=1, device_id={Z: to_z(d)}, device_id_type=pl.DeviceIdType.MESH)
    for d in range(1, ny):
        pl.semaphore_signal(barrier, inc=1, device_id={Y: lax.rem(y + d, ny)}, device_id_type=pl.DeviceIdType.MESH)
    for k in range(1, nx * nc):
        pl.semaphore_signal(barrier, inc=1, device_id=col_peer(k), device_id_type=pl.DeviceIdType.MESH)
    for copy in local:
        copy.start()
    for copy in local:
        copy.wait()
    weight_sq = jnp.sum(wv[...] * wv[...], axis=0, keepdims=True)
    weight_sq = sum(weight_sq[:, g * LANE:(g + 1) * LANE] for g in range(groups))
    st2[y, 8:16, :] = jnp.broadcast_to(weight_sq, (8, LANE))
    pl.semaphore_wait(barrier, nz - 1 + ny - 1 + nx * nc - 1)

    own_rows = pl.ds(pl.multiple_of(own, share), share)
    core_part = pl.ds(pl.multiple_of(c * core_rows, core_rows), core_rows)
    sibling = {C: nc - 1 - c}

    def send_acts(target, i, q, send, recv):
        there = pl.ds(pl.multiple_of(target * rows_z, LANE), rows_z)
        remote(acts.at[own_rows, there], A.at[i, q, own_rows, :], send, recv, {Z: target}).start()

    def last_hop(way, g):
        return half if (g % 2 == 0) == (way == 0) else half - 1

    def ring_copy(way, g, h):
        src = G.at[g, h - 1, way] if h else G.at[g, far, 0]
        q = 1 if h + 1 == half else way
        return remote(
            src, G.at[g, h, q], ring_send.at[way, 0 if last_hop(way, g) == half else 1],
            ring_recv.at[way, g, h], {Z: to_z(1 if way == 0 else nz - 1)},
        )

    def pairs_stage(stage, pairs):
        i, n = pairs[0], len(pairs)
        if pairs == [far]:
            block, kind = (lambda rows: A.at[far, 1, rows, :]), 1
        else:
            block, kind = (lambda rows: A.at[pl.ds(i, n), :, rows, :]), 0
        if stage == 1:
            for j in pairs:
                wait_bytes(A.at[far, 1, pl.ds(0, share), :] if kind else A.at[0, :, pl.ds(0, share), :], a2a_recv.at[j])
            for d in range(1, nx):
                remote(block(own_rows), block(own_rows), x_send.at[kind], x_recv.at[i], {X: lax.rem(x + d, nx)}).start()
        elif stage == 2:
            wait_bytes(block(pl.ds(0, share * (nx - 1))), x_recv.at[i])
            remote(block(core_part), block(core_part), d_send.at[kind], d_recv.at[i], sibling).start()
        else:
            wait_bytes(block(pl.ds(0, core_rows)), d_recv.at[i])

    started = set()
    for what, *of in plan(half, groups, LAG, BATCHES):
        if what == "first":
            for way in range(2):
                ring_copy(way, of[0], 0).start()
        elif what == "acts":
            for h in range(1, half):
                send_acts(to_z(h), h - 1, 0, a2a_send.at[0], a2a_recv.at[h - 1])
                send_acts(to_z(nz - h), h - 1, 1, a2a_send.at[0], a2a_recv.at[h - 1])
            send_acts(to_z(half), far, 1, a2a_send.at[1], a2a_recv.at[far])
        elif what == "hop":
            g, h = of
            for way in range(2):
                if h <= last_hop(way, g):
                    wait_bytes(G.at[g, 0, 0], ring_recv.at[way, g, h - 1])
                if h < last_hop(way, g):
                    ring_copy(way, g, h).start()
        elif what == "pairs":
            pairs_stage(*of)
        elif what == "dot":
            g, todo = of
            for i in todo:
                product = lax.dot_general(
                    G[g, i].reshape(2 * tok, LANE), A[i].reshape(2 * tok, rows_z),
                    (((0,), (0,)), ((), ())), preferred_element_type=jnp.float32,
                )
                for yy in range(ny):
                    block = product[:, yy * LANE:(yy + 1) * LANE]
                    part[g, yy] = part[g, yy] + block if g in started else block
                started.add(g)
        elif what == "scatter":
            g = of[0]
            for d in range(1, ny):
                there = lax.rem(y + d, ny)
                remote(part.at[g, there], R.at[g, d - 1], y_send.at[0], y_recv.at[g], {Y: there}).start()

    row_sq = jnp.zeros((1, LANE), jnp.float32)
    for g in range(groups):
        wait_bytes(R.at[0], y_recv.at[g])
        total = part[g, y]
        for d in range(ny - 1):
            total += R[g, d]
        row_sq += jnp.sum(total * total + floor_eps, axis=0, keepdims=True)
        grad[:, g * LANE:(g + 1) * LANE] = total.T

    st1[xc] = jnp.broadcast_to(row_sq, (8, LANE))
    for k in range(1, nx * nc):
        remote(st1.at[xc], st1.at[xc], st_send.at[0], st_recv.at[0], col_peer(k)).start()
    for g in range(groups):
        grads = grad[:, g * LANE:(g + 1) * LANE]
        st2[y, g:g + 1, :] = jnp.sum(grads * grads + floor_eps, axis=0, keepdims=True)
    wait_bytes(A.at[pl.ds(0, half - 1), :, pl.ds(0, share), :], a2a_send.at[0])
    wait_bytes(A.at[0, 0, pl.ds(0, share), :], a2a_send.at[1])
    wait_bytes(A.at[pl.ds(0, half - 1), :, pl.ds(0, share * (nx - 1)), :], x_send.at[0])
    wait_bytes(A.at[0, 0, pl.ds(0, share * (nx - 1)), :], x_send.at[1])
    wait_bytes(A.at[pl.ds(0, half - 1), :, pl.ds(0, core_rows), :], d_send.at[0])
    wait_bytes(A.at[0, 0, pl.ds(0, core_rows), :], d_send.at[1])
    for way in range(2):
        wait_bytes(G.at[0], ring_send.at[way, 0])
        wait_bytes(G.at[0, pl.ds(0, half - 1)], ring_send.at[way, 1])
    wait_bytes(part.at[:, pl.ds(0, ny - 1)], y_send.at[0])

    wait_bytes(st1.at[pl.ds(0, nx * nc - 1)], st_recv.at[0])
    row_total = st1[0, 0:1, :]
    for k in range(1, nx * nc):
        row_total += st1[k, 0:1, :]
    row_moment = decay_rate * rs_v[...] + (1.0 - decay_rate) * (row_total / cols_all)
    row_out[...] = row_moment
    rows_down = jnp.broadcast_to(row_moment, (LANE, LANE)).T
    inverse = 1.0 / rows_down
    for g in range(groups):
        grads = grad[:, g * LANE:(g + 1) * LANE]
        st2[y, 4 + g:5 + g, :] = jnp.sum(grads * grads * inverse, axis=0, keepdims=True)

    for d in range(1, ny):
        remote(st2.at[y], st2.at[y], st_send.at[1], st_recv.at[1], {Y: lax.rem(y + d, ny)}).start()
    wait_bytes(st1.at[pl.ds(0, nx * nc - 1)], st_send.at[0])
    wait_bytes(st2.at[pl.ds(0, ny - 1)], st_recv.at[1])
    over_y = st2[0]
    for d in range(1, ny):
        over_y += st2[d]
    st3[z] = over_y
    for d in sorted(range(1, nz), key=lambda d: -min(d, nz - d)):
        remote(st3.at[z], st3.at[z], st_send.at[2], st_recv.at[2], {Z: to_z(d)}).start()
    wait_bytes(st2.at[pl.ds(0, ny - 1)], st_send.at[1])
    wait_bytes(st3.at[pl.ds(0, nz - 1)], st_recv.at[2])
    over_z = st3[0]
    for d in range(1, nz):
        over_z += st3[d]
    col_moment = decay_rate * cs_v[...] + (1.0 - decay_rate) * (over_z[0:groups] / width)
    st4[xc, 0:4, :] = over_z[4:4 + groups] / col_moment
    st4[xc, 4:8, :] = over_z[8:12]

    for k in range(1, nx * nc):
        remote(st4.at[xc], st4.at[xc], st_send.at[3], st_recv.at[3], col_peer(k)).start()
    col_out[...] = col_moment
    for g in range(groups):
        lanes = slice(g * LANE, (g + 1) * LANE)
        unclipped_out[:, lanes] = grad[:, lanes] * lax.rsqrt(rows_down * col_moment[g:g + 1, :])
    wait_bytes(st3.at[pl.ds(0, nz - 1)], st_send.at[2])
    wait_bytes(st4.at[pl.ds(0, nx * nc - 1)], st_recv.at[3])
    over_x = st4[0]
    for k in range(1, nx * nc):
        over_x += st4[k]
    update_total = jnp.sum(over_x[0:4], keepdims=True)
    weight_total = jnp.sum(over_x[4:5], keepdims=True)
    clip_out[...] = jnp.broadcast_to(jnp.maximum(1.0, jnp.sqrt(update_total / count_all)), clip_out.shape)
    step_out[...] = jnp.broadcast_to(relative_rate * jnp.sqrt(weight_total / count_all + 1e-06), step_out.shape)
    wait_bytes(st4.at[pl.ds(0, nx * nc - 1)], st_send.at[3])


def per_device(acts, out_grads, weight, row_state, col_state):
    nz, ny, nx, nc = (lax.axis_size(a) for a in (Z, Y, X, C))
    tok, width = acts.shape
    cols = out_grads.shape[1]
    groups = cols // LANE
    half = nz // 2
    rows_z = ny * LANE
    anywhere = pl.BlockSpec(memory_space=pl.ANY)
    vmem = pl.BlockSpec(memory_space=pltpu.VMEM)
    f32 = jnp.float32
    unclipped, row_moment, col_moment, clip_factor, step_size = pl.pallas_call(
        functools.partial(kernel, (nz, ny, nx, nc, tok, cols, width)),
        out_shape=(
            jax.ShapeDtypeStruct((LANE, cols), f32),
            jax.ShapeDtypeStruct((1, LANE), f32),
            jax.ShapeDtypeStruct((groups, LANE), f32),
            jax.ShapeDtypeStruct((groups, LANE), f32),
            jax.ShapeDtypeStruct((groups, LANE), f32),
        ),
        in_specs=[anywhere] * 5,
        out_specs=[vmem] * 5,
        scratch_shapes=[
            pltpu.VMEM((half, 2, tok, rows_z), jnp.bfloat16),
            pltpu.VMEM((groups, half, 2, tok, LANE), jnp.bfloat16),
            pltpu.VMEM((groups, ny, LANE, LANE), f32),
            pltpu.VMEM((groups, ny - 1, LANE, LANE), f32),
            pltpu.VMEM((LANE, cols), f32),
            pltpu.VMEM((LANE, cols), f32),
            pltpu.VMEM((1, LANE), f32),
            pltpu.VMEM((groups, LANE), f32),
            pltpu.VMEM((nx * nc, 8, LANE), f32),
            pltpu.VMEM((ny, 16, LANE), f32),
            pltpu.VMEM((nz, 16, LANE), f32),
            pltpu.VMEM((nx * nc, 8, LANE), f32),
            pltpu.SemaphoreType.DMA((groups + 4,)),
            pltpu.SemaphoreType.DMA((2,)),
            pltpu.SemaphoreType.DMA((half,)),
            pltpu.SemaphoreType.DMA((2,)),
            pltpu.SemaphoreType.DMA((half,)),
            pltpu.SemaphoreType.DMA((2,)),
            pltpu.SemaphoreType.DMA((half,)),
            pltpu.SemaphoreType.DMA((2, 2)),
            pltpu.SemaphoreType.DMA((2, groups, half)),
            pltpu.SemaphoreType.DMA((1,)),
            pltpu.SemaphoreType.DMA((groups,)),
            pltpu.SemaphoreType.DMA((4,)),
            pltpu.SemaphoreType.DMA((4,)),
        ],
        compiler_params=pltpu.CompilerParams(
            collective_id=0, has_side_effects=True, vmem_limit_bytes=60 * 1024 * 1024
        ),
    )(acts, out_grads, weight, row_state.reshape(1, LANE), col_state.reshape(groups, LANE))
    update = unclipped / clip_factor.reshape(1, -1)
    new_weight = weight - step_size.reshape(1, -1) * update
    return (new_weight, update, row_moment.reshape(-1), col_moment.reshape(-1))


def solution(mesh):
    finer = Mesh(mesh.devices.reshape(16, 4, 4, 2), (Z, Y, X, C))
    return jax.shard_map(
        per_device,
        mesh=finer,
        in_specs=(P(ROW, None), P(ROW, COL), P(ROW, COL), P(ROW), P(COL)),
        out_specs=(P(ROW, COL), P(ROW, COL), P(ROW), P(COL)),
        check_vma=False,
    )
```

```python
import functools

import jax
import jax.numpy as jnp
from jax import lax
from jax.experimental import pallas as pl
from jax.experimental.pallas import tpu as pltpu
from jax.sharding import Mesh
from jax.sharding import PartitionSpec as P

Z, Y, X, C = "z", "y", "x", "c"
ROW = (Z, Y)
COL = (X, C)
LANE = 128
LAG = (0, 0, 1, 1)
SENDS = (([7], 0), ([6, 5], 0), ([4, 3], 1), ([2, 1, 0], 2))
BATCHES = (([7], 2), ([5, 6], 2), ([3, 4], 3), ([0, 1, 2], 4))

decay_rate = 0.85
floor_eps = 1e-30
relative_rate = 0.05


def plan(half, groups, lag, sends, batches):
    steps = [("first", g) for g in range(groups) if lag[g] == 0]
    steps += [("acts", pairs) for pairs, at in sends if at == 0]
    steps.append(("weights",))
    steps += [("first", g) for g in range(groups) if lag[g] == 1]
    ready, done = [], {g: [] for g in range(groups)}
    arrived = {g: [] for g in range(groups)}
    for r in range(1, half + max(lag) + 1):
        for g in range(groups):
            if lag[g] == r and r > 1:
                steps.append(("first", g))
            h = r - lag[g]
            if 1 <= h <= half:
                steps.append(("hop", g, h))
                arrived[g].append(h - 1)
        steps += [("acts", pairs) for pairs, at in sends if at == r]
        for stage in (1, 2, 3):
            for pairs, at in batches:
                if at + stage - 1 == r:
                    steps.append(("pairs", stage, pairs))
                    if stage == 3:
                        ready += pairs
        for g in range(groups):
            todo = [i for i in arrived[g] if i in ready and i not in done[g]]
            done[g] += todo
            if todo:
                steps.append(("dot", g, todo))
            if r - lag[g] == half:
                assert len(done[g]) == half
                steps.append(("scatter", g))
    return steps


def kernel(
    sizes,
    acts, og, weight, row_state, col_state,
    unclipped_out, row_out, col_out, clip_out, step_out,
    A, G, part, R, grad, wv, rs_v, cs_v, st1, st2, st3, st4, wy, wz,
    local_sem, a2a_send, a2a_recv, x_send, x_recv, d_send, d_recv,
    ring_send, ring_recv, y_send, y_recv, st_send, st_recv,
):
    nz, ny, nx, nc, tok, cols, width = sizes
    half = nz // 2
    groups = cols // LANE
    rows_z = ny * LANE
    share = tok // (nx * nc)
    core_rows = share * nx
    cols_all = cols * nx * nc
    count_all = width * cols_all
    z, y, x, c = (lax.axis_index(a) for a in (Z, Y, X, C))
    xc = x * nc + c
    own = c * core_rows + x * share
    far = half - 1

    def to_z(d):
        return lax.rem(z + d, nz)

    def remote(src, dst, send, recv, where):
        return pltpu.make_async_remote_copy(
            src_ref=src, dst_ref=dst, send_sem=send, recv_sem=recv,
            device_id=where, device_id_type=pl.DeviceIdType.MESH,
        )

    def wait_bytes(ref, sem):
        pltpu.make_async_copy(ref, ref, sem).wait()

    ys = sorted(range(1, ny), key=lambda d: -min(d, ny - d))
    xs = sorted(range(1, nx), key=lambda d: -min(d, nx - d))
    zs = sorted(range(1, nz), key=lambda d: -min(d, nz - d))
    peers = [(d, e) for d in xs for e in range(nc)] + [(0, e) for e in range(1, nc)]

    def col_peer(k):
        d, e = k
        return {X: lax.rem(x + d, nx), C: lax.rem(c + e, nc)}

    own_cols = pl.ds(pl.multiple_of(z * rows_z, LANE), rows_z)
    local = [
        pltpu.make_async_copy(og.at[:, pl.ds(g * LANE, LANE)], G.at[g, far, 0], local_sem.at[g])
        for g in range(groups)
    ] + [
        pltpu.make_async_copy(acts.at[:, own_cols], A.at[far, 0], local_sem.at[groups]),
        pltpu.make_async_copy(weight, wv, local_sem.at[groups + 1]),
        pltpu.make_async_copy(row_state, rs_v, local_sem.at[groups + 2]),
        pltpu.make_async_copy(col_state, cs_v, local_sem.at[groups + 3]),
    ]

    barrier = pltpu.get_barrier_semaphore()
    for d in zs:
        pl.semaphore_signal(barrier, inc=1, device_id={Z: to_z(d)}, device_id_type=pl.DeviceIdType.MESH)
    for d in range(1, ny):
        pl.semaphore_signal(barrier, inc=1, device_id={Y: lax.rem(y + d, ny)}, device_id_type=pl.DeviceIdType.MESH)
    for k in peers:
        pl.semaphore_signal(barrier, inc=1, device_id=col_peer(k), device_id_type=pl.DeviceIdType.MESH)
    for copy in local:
        copy.start()
    for copy in local:
        copy.wait()
    weight_sq = jnp.sum(wv[...] * wv[...], axis=0, keepdims=True)
    weight_sq = sum(weight_sq[:, g * LANE:(g + 1) * LANE] for g in range(groups))
    wy[y] = weight_sq
    pl.semaphore_wait(barrier, nz - 1 + ny - 1 + nx * nc - 1)

    own_rows = pl.ds(pl.multiple_of(own, share), share)
    core_part = pl.ds(pl.multiple_of(c * core_rows, core_rows), core_rows)
    sibling = {C: nc - 1 - c}

    def send_acts(target, i, q, send, recv):
        there = pl.ds(pl.multiple_of(target * rows_z, LANE), rows_z)
        remote(acts.at[own_rows, there], A.at[i, q, own_rows, :], send, recv, {Z: target}).start()

    def last_hop(way, g):
        return half if (g % 2 == 0) == (way == 0) else half - 1

    def ring_copy(way, g, h):
        src = G.at[g, h - 1, way] if h else G.at[g, far, 0]
        q = 1 if h + 1 == half else way
        return remote(
            src, G.at[g, h, q], ring_send.at[way, 0 if last_hop(way, g) == half else 1],
            ring_recv.at[way, g, h], {Z: to_z(1 if way == 0 else nz - 1)},
        )

    def pairs_stage(stage, pairs):
        i, n = pairs[0], len(pairs)
        if pairs == [far]:
            block, kind = (lambda rows: A.at[far, 1, rows, :]), 1
        else:
            block, kind = (lambda rows: A.at[pl.ds(i, n), :, rows, :]), 0
        if stage == 1:
            for j in pairs:
                wait_bytes(A.at[far, 1, pl.ds(0, share), :] if kind else A.at[0, :, pl.ds(0, share), :], a2a_recv.at[j])
            for d in xs:
                remote(block(own_rows), block(own_rows), x_send.at[kind], x_recv.at[i], {X: lax.rem(x + d, nx)}).start()
        elif stage == 2:
            wait_bytes(block(pl.ds(0, share * (nx - 1))), x_recv.at[i])
            remote(block(core_part), block(core_part), d_send.at[kind], d_recv.at[i], sibling).start()
        else:
            wait_bytes(block(pl.ds(0, core_rows)), d_recv.at[i])

    def weights_over_y():
        for d in range(1, ny):
            remote(wy.at[y], wy.at[y], st_send.at[4], st_recv.at[4], {Y: lax.rem(y + d, ny)}).start()

    def weights_over_z():
        wait_bytes(wy.at[pl.ds(0, ny - 1)], st_recv.at[4])
        here = wy[0]
        for d in range(1, ny):
            here += wy[d]
        wz[z] = here
        for d in range(1, nz):
            remote(wz.at[z], wz.at[z], st_send.at[5], st_recv.at[5], {Z: to_z(d)}).start()

    started = set()
    for what, *of in plan(half, groups, LAG, SENDS, BATCHES):
        if what == "first":
            for way in range(2):
                ring_copy(way, of[0], 0).start()
        elif what == "acts":
            for i in of[0]:
                if i == far:
                    send_acts(to_z(half), far, 1, a2a_send.at[1], a2a_recv.at[far])
                else:
                    send_acts(to_z(i + 1), i, 0, a2a_send.at[0], a2a_recv.at[i])
                    send_acts(to_z(nz - 1 - i), i, 1, a2a_send.at[0], a2a_recv.at[i])
        elif what == "weights":
            weights_over_y()
        elif what == "hop":
            g, h = of
            if h == half - 1 and g == 0:
                weights_over_z()
            for way in range(2):
                if h <= last_hop(way, g):
                    wait_bytes(G.at[g, 0, 0], ring_recv.at[way, g, h - 1])
                if h < last_hop(way, g):
                    ring_copy(way, g, h).start()
        elif what == "pairs":
            pairs_stage(*of)
        elif what == "dot":
            g, todo = of
            for i in todo:
                product = lax.dot_general(
                    G[g, i].reshape(2 * tok, LANE), A[i].reshape(2 * tok, rows_z),
                    (((0,), (0,)), ((), ())), preferred_element_type=jnp.float32,
                )
                for yy in range(ny):
                    block = product[:, yy * LANE:(yy + 1) * LANE]
                    part[g, yy] = part[g, yy] + block if g in started else block
                started.add(g)
        elif what == "scatter":
            g = of[0]
            for d in ys:
                there = lax.rem(y + d, ny)
                remote(part.at[g, there], R.at[g, d - 1], y_send.at[0], y_recv.at[g], {Y: there}).start()

    row_sq = jnp.zeros((1, LANE), jnp.float32)
    for g in range(groups):
        if g == groups - 1:
            wait_bytes(A.at[pl.ds(0, half - 1), :, pl.ds(0, share), :], a2a_send.at[0])
            wait_bytes(A.at[0, 0, pl.ds(0, share), :], a2a_send.at[1])
            wait_bytes(A.at[pl.ds(0, half - 1), :, pl.ds(0, share * (nx - 1)), :], x_send.at[0])
            wait_bytes(A.at[0, 0, pl.ds(0, share * (nx - 1)), :], x_send.at[1])
            wait_bytes(A.at[pl.ds(0, half - 1), :, pl.ds(0, core_rows), :], d_send.at[0])
            wait_bytes(A.at[0, 0, pl.ds(0, core_rows), :], d_send.at[1])
            for way in range(2):
                wait_bytes(G.at[0], ring_send.at[way, 0])
                wait_bytes(G.at[0, pl.ds(0, half - 1)], ring_send.at[way, 1])
            wait_bytes(wy.at[pl.ds(0, ny - 1)], st_send.at[4])
            wait_bytes(wz.at[pl.ds(0, nz - 1)], st_send.at[5])
            wait_bytes(wz.at[pl.ds(0, nz - 1)], st_recv.at[5])
        wait_bytes(R.at[0], y_recv.at[g])
        total = part[g, y]
        for d in range(ny - 1):
            total += R[g, d]
        row_sq += jnp.sum(total * total + floor_eps, axis=0, keepdims=True)
        if g < groups - 1:
            grad[:, g * LANE:(g + 1) * LANE] = total.T

    st1[xc] = jnp.broadcast_to(row_sq, (8, LANE))
    for k in peers:
        remote(st1.at[xc], st1.at[xc], st_send.at[0], st_recv.at[0], col_peer(k)).start()
    grad[:, (groups - 1) * LANE:] = total.T
    for g in range(groups):
        grads = grad[:, g * LANE:(g + 1) * LANE]
        st2[y, g:g + 1, :] = jnp.sum(grads * grads + floor_eps, axis=0, keepdims=True)
    weight_total = wz[0]
    for d in range(1, nz):
        weight_total += wz[d]
    st4[xc, 4:8, :] = jnp.broadcast_to(weight_total, (4, LANE))
    wait_bytes(part.at[:, pl.ds(0, ny - 1)], y_send.at[0])
    wait_bytes(st1.at[pl.ds(0, nx * nc - 1)], st_send.at[0])

    wait_bytes(st1.at[pl.ds(0, nx * nc - 1)], st_recv.at[0])
    row_total = st1[0, 0:1, :]
    for k in range(1, nx * nc):
        row_total += st1[k, 0:1, :]
    row_moment = decay_rate * rs_v[...] + (1.0 - decay_rate) * (row_total / cols_all)
    inverse = jnp.broadcast_to(1.0 / row_moment, (LANE, LANE)).T
    for g in range(groups):
        grads = grad[:, g * LANE:(g + 1) * LANE]
        st2[y, 4 + g:5 + g, :] = jnp.sum(grads * grads * inverse, axis=0, keepdims=True)

    for d in ys:
        remote(st2.at[y], st2.at[y], st_send.at[1], st_recv.at[1], {Y: lax.rem(y + d, ny)}).start()
    row_out[...] = row_moment
    rows_down = jnp.broadcast_to(row_moment, (LANE, LANE)).T
    wait_bytes(st2.at[pl.ds(0, ny - 1)], st_send.at[1])
    wait_bytes(st2.at[pl.ds(0, ny - 1)], st_recv.at[1])
    over_y = st2[0]
    for d in range(1, ny):
        over_y += st2[d]
    st3[z] = over_y
    for d in zs:
        remote(st3.at[z], st3.at[z], st_send.at[2], st_recv.at[2], {Z: to_z(d)}).start()
    wait_bytes(st3.at[pl.ds(0, nz - 1)], st_send.at[2])
    wait_bytes(st3.at[pl.ds(0, nz - 1)], st_recv.at[2])
    over_z = st3[0]
    for d in range(1, nz):
        over_z += st3[d]
    col_moment = decay_rate * cs_v[...] + (1.0 - decay_rate) * (over_z[0:groups] / width)
    st4[xc, 0:4, :] = over_z[4:4 + groups] / col_moment

    for k in peers:
        remote(st4.at[xc], st4.at[xc], st_send.at[3], st_recv.at[3], col_peer(k)).start()
    col_out[...] = col_moment
    for g in range(groups):
        lanes = slice(g * LANE, (g + 1) * LANE)
        unclipped_out[:, lanes] = grad[:, lanes] * lax.rsqrt(rows_down * col_moment[g:g + 1, :])
    wait_bytes(st4.at[pl.ds(0, nx * nc - 1)], st_recv.at[3])
    over_x = st4[0]
    for k in range(1, nx * nc):
        over_x += st4[k]
    update_total = jnp.sum(over_x[0:4], keepdims=True)
    weight_total = jnp.sum(over_x[4:5], keepdims=True)
    clip_out[...] = jnp.broadcast_to(jnp.maximum(1.0, jnp.sqrt(update_total / count_all)), clip_out.shape)
    step_out[...] = jnp.broadcast_to(relative_rate * jnp.sqrt(weight_total / count_all + 1e-06), step_out.shape)
    wait_bytes(st4.at[pl.ds(0, nx * nc - 1)], st_send.at[3])


def finish(unclipped, weight, row_moment, col_moment, clip_factor, step_size, new_weight, update, row_out, col_out):
    row_out[...] = row_moment[...]
    col_out[...] = col_moment[...]
    for g in range(col_moment.shape[0]):
        lanes = slice(g * LANE, (g + 1) * LANE)
        clipped = unclipped[:, lanes] / clip_factor[g:g + 1, :]
        update[:, lanes] = clipped
        new_weight[:, lanes] = weight[:, lanes] - step_size[g:g + 1, :] * clipped


def per_device(acts, out_grads, weight, row_state, col_state):
    nz, ny, nx, nc = (lax.axis_size(a) for a in (Z, Y, X, C))
    tok, width = acts.shape
    cols = out_grads.shape[1]
    groups = cols // LANE
    half = nz // 2
    rows_z = ny * LANE
    anywhere = pl.BlockSpec(memory_space=pl.ANY)
    vmem = pl.BlockSpec(memory_space=pltpu.VMEM)
    f32 = jnp.float32
    unclipped, row_moment, col_moment, clip_factor, step_size = pl.pallas_call(
        functools.partial(kernel, (nz, ny, nx, nc, tok, cols, width)),
        out_shape=(
            jax.ShapeDtypeStruct((LANE, cols), f32),
            jax.ShapeDtypeStruct((1, LANE), f32),
            jax.ShapeDtypeStruct((groups, LANE), f32),
            jax.ShapeDtypeStruct((groups, LANE), f32),
            jax.ShapeDtypeStruct((groups, LANE), f32),
        ),
        in_specs=[anywhere] * 5,
        out_specs=[vmem] * 5,
        scratch_shapes=[
            pltpu.VMEM((half, 2, tok, rows_z), jnp.bfloat16),
            pltpu.VMEM((groups, half, 2, tok, LANE), jnp.bfloat16),
            pltpu.VMEM((groups, ny, LANE, LANE), f32),
            pltpu.VMEM((groups, ny - 1, LANE, LANE), f32),
            pltpu.VMEM((LANE, cols), f32),
            pltpu.VMEM((LANE, cols), f32),
            pltpu.VMEM((1, LANE), f32),
            pltpu.VMEM((groups, LANE), f32),
            pltpu.VMEM((nx * nc, 8, LANE), f32),
            pltpu.VMEM((ny, 8, LANE), f32),
            pltpu.VMEM((nz, 8, LANE), f32),
            pltpu.VMEM((nx * nc, 8, LANE), f32),
            pltpu.VMEM((ny, 1, LANE), f32),
            pltpu.VMEM((nz, 1, LANE), f32),
            pltpu.SemaphoreType.DMA((groups + 4,)),
            pltpu.SemaphoreType.DMA((2,)),
            pltpu.SemaphoreType.DMA((half,)),
            pltpu.SemaphoreType.DMA((2,)),
            pltpu.SemaphoreType.DMA((half,)),
            pltpu.SemaphoreType.DMA((2,)),
            pltpu.SemaphoreType.DMA((half,)),
            pltpu.SemaphoreType.DMA((2, 2)),
            pltpu.SemaphoreType.DMA((2, groups, half)),
            pltpu.SemaphoreType.DMA((1,)),
            pltpu.SemaphoreType.DMA((groups,)),
            pltpu.SemaphoreType.DMA((6,)),
            pltpu.SemaphoreType.DMA((6,)),
        ],
        compiler_params=pltpu.CompilerParams(
            collective_id=0, has_side_effects=True, vmem_limit_bytes=60 * 1024 * 1024
        ),
    )(acts, out_grads, weight, row_state.reshape(1, LANE), col_state.reshape(groups, LANE))
    new_weight, update, row_moment, col_moment = pl.pallas_call(
        finish,
        out_shape=(
            jax.ShapeDtypeStruct((LANE, cols), f32),
            jax.ShapeDtypeStruct((LANE, cols), f32),
            jax.ShapeDtypeStruct((1, LANE), f32),
            jax.ShapeDtypeStruct((groups, LANE), f32),
        ),
        in_specs=[vmem] * 6,
        out_specs=[vmem] * 4,
    )(unclipped, weight, row_moment, col_moment, clip_factor, step_size)
    return (new_weight, update, row_moment.reshape(-1), col_moment.reshape(-1))


def solution(mesh):
    finer = Mesh(mesh.devices.reshape(16, 4, 4, 2), (Z, Y, X, C))
    return jax.shard_map(
        per_device,
        mesh=finer,
        in_specs=(P(ROW, None), P(ROW, COL), P(ROW, COL), P(ROW), P(COL)),
        out_specs=(P(ROW, COL), P(ROW, COL), P(ROW), P(COL)),
        check_vma=False,
    )
```

```python
import functools

import jax
import jax.numpy as jnp
from jax import lax
from jax.experimental import pallas as pl
from jax.experimental.pallas import tpu as pltpu
from jax.sharding import Mesh
from jax.sharding import PartitionSpec as P

Z, Y, X, C = "z", "y", "x", "c"
ROW = (Z, Y)
COL = (X, C)
LANE = 128
LAG = (0, 0, 1, 2)
SENDS = (([7], 0), ([6], 1), ([5], 1), ([4], 2), ([3], 2), ([2], 2), ([1], 3), ([0], 3))
BATCHES = (([7], 2), ([5, 6], 3), ([2, 3, 4], 4), ([0, 1], 5))

decay_rate = 0.85
floor_eps = 1e-30
relative_rate = 0.05


def plan(half, groups, lag, sends, batches):
    steps = [("first", g) for g in range(groups) if lag[g] == 0]
    steps += [("acts", pairs) for pairs, at in sends if at == 0]
    steps.append(("weights",))
    steps += [("first", g) for g in range(groups) if lag[g] == 1]
    ready, done = [], {g: [] for g in range(groups)}
    arrived = {g: [] for g in range(groups)}

    def multiply(g):
        todo = [i for i in arrived[g] if i in ready and i not in done[g]]
        done[g] += todo
        if todo:
            steps.append(("dot", g, todo))
        if len(done[g]) == half:
            steps.append(("scatter", g))

    for r in range(1, half + max(lag) + 1):
        for g in range(groups):
            if lag[g] == r and r > 1:
                steps.append(("first", g))
            h = r - lag[g]
            if 1 <= h <= half:
                steps.append(("hop", g, h))
                arrived[g].append(h - 1)
                if h == half and len(ready) == half:
                    multiply(g)
        steps += [("acts", pairs) for pairs, at in sends if at == r]
        for stage in (1, 2, 3):
            for pairs, at in batches:
                if at + stage - 1 == r:
                    steps.append(("pairs", stage, pairs))
                    if stage == 3:
                        ready += pairs
        for g in range(groups):
            if len(done[g]) < half:
                multiply(g)
    assert all(len(done[g]) == half for g in range(groups))
    return steps


def kernel(
    sizes,
    acts, og, weight, row_state, col_state,
    unclipped_out, row_out, col_out, clip_out, step_out,
    A, G, part, R, grad, wv, rs_v, cs_v, st1, st2, st3, st4, wy, wz,
    local_sem, a2a_send, a2a_recv, x_send, x_recv, d_send, d_recv,
    ring_send, ring_recv, y_send, y_recv, st_send, st_recv,
):
    nz, ny, nx, nc, tok, cols, width = sizes
    half = nz // 2
    groups = cols // LANE
    rows_z = ny * LANE
    share = tok // (nx * nc)
    core_rows = share * nx
    cols_all = cols * nx * nc
    count_all = width * cols_all
    z, y, x, c = (lax.axis_index(a) for a in (Z, Y, X, C))
    xc = x * nc + c
    own = c * core_rows + x * share
    far = half - 1

    def to_z(d):
        return lax.rem(z + d, nz)

    def remote(src, dst, send, recv, where):
        return pltpu.make_async_remote_copy(
            src_ref=src, dst_ref=dst, send_sem=send, recv_sem=recv,
            device_id=where, device_id_type=pl.DeviceIdType.MESH,
        )

    def wait_bytes(ref, sem):
        pltpu.make_async_copy(ref, ref, sem).wait()

    ys = sorted(range(1, ny), key=lambda d: -min(d, ny - d))
    xs = sorted(range(1, nx), key=lambda d: -min(d, nx - d))
    zs = sorted(range(1, nz), key=lambda d: -min(d, nz - d))
    peers = [(d, e) for d in xs for e in range(nc)] + [(0, e) for e in range(1, nc)]

    def col_peer(k):
        d, e = k
        return {X: lax.rem(x + d, nx), C: lax.rem(c + e, nc)}

    own_cols = pl.ds(pl.multiple_of(z * rows_z, LANE), rows_z)
    local = [
        pltpu.make_async_copy(og.at[:, pl.ds(g * LANE, LANE)], G.at[g, far, 0], local_sem.at[g])
        for g in range(groups)
    ] + [
        pltpu.make_async_copy(acts.at[:, own_cols], A.at[far, 0], local_sem.at[groups]),
        pltpu.make_async_copy(weight, wv, local_sem.at[groups + 1]),
        pltpu.make_async_copy(row_state, rs_v, local_sem.at[groups + 2]),
        pltpu.make_async_copy(col_state, cs_v, local_sem.at[groups + 3]),
    ]

    barrier = pltpu.get_barrier_semaphore()
    for d in zs:
        pl.semaphore_signal(barrier, inc=1, device_id={Z: to_z(d)}, device_id_type=pl.DeviceIdType.MESH)
    for d in range(1, ny):
        pl.semaphore_signal(barrier, inc=1, device_id={Y: lax.rem(y + d, ny)}, device_id_type=pl.DeviceIdType.MESH)
    for k in peers:
        pl.semaphore_signal(barrier, inc=1, device_id=col_peer(k), device_id_type=pl.DeviceIdType.MESH)
    for copy in local:
        copy.start()
    for copy in local:
        copy.wait()
    weight_sq = jnp.sum(wv[...] * wv[...], axis=0, keepdims=True)
    weight_sq = sum(weight_sq[:, g * LANE:(g + 1) * LANE] for g in range(groups))
    wy[y] = weight_sq
    pl.semaphore_wait(barrier, nz - 1 + ny - 1 + nx * nc - 1)

    own_rows = pl.ds(pl.multiple_of(own, share), share)
    core_part = pl.ds(pl.multiple_of(c * core_rows, core_rows), core_rows)
    sibling = {C: nc - 1 - c}

    def send_acts(target, i, q, send, recv):
        there = pl.ds(pl.multiple_of(target * rows_z, LANE), rows_z)
        remote(acts.at[own_rows, there], A.at[i, q, own_rows, :], send, recv, {Z: target}).start()

    def last_hop(way, g):
        return half if (g % 2 == 0) == (way == 0) else half - 1

    def ring_copy(way, g, h):
        src = G.at[g, h - 1, way] if h else G.at[g, far, 0]
        q = 1 if h + 1 == half else way
        return remote(
            src, G.at[g, h, q], ring_send.at[way, 0 if last_hop(way, g) == half else 1],
            ring_recv.at[way, g, h], {Z: to_z(1 if way == 0 else nz - 1)},
        )

    def pairs_stage(stage, pairs):
        i, n = pairs[0], len(pairs)
        if pairs == [far]:
            block, kind = (lambda rows: A.at[far, 1, rows, :]), 1
        else:
            block, kind = (lambda rows: A.at[pl.ds(i, n), :, rows, :]), 0
        if stage == 1:
            for j in pairs:
                wait_bytes(A.at[far, 1, pl.ds(0, share), :] if kind else A.at[0, :, pl.ds(0, share), :], a2a_recv.at[j])
            for d in xs:
                remote(block(own_rows), block(own_rows), x_send.at[kind], x_recv.at[i], {X: lax.rem(x + d, nx)}).start()
        elif stage == 2:
            wait_bytes(block(pl.ds(0, share * (nx - 1))), x_recv.at[i])
            remote(block(core_part), block(core_part), d_send.at[kind], d_recv.at[i], sibling).start()
        else:
            wait_bytes(block(pl.ds(0, core_rows)), d_recv.at[i])

    def weights_over_y():
        for d in range(1, ny):
            remote(wy.at[y], wy.at[y], st_send.at[4], st_recv.at[4], {Y: lax.rem(y + d, ny)}).start()

    def weights_over_z():
        wait_bytes(wy.at[pl.ds(0, ny - 1)], st_recv.at[4])
        here = wy[0]
        for d in range(1, ny):
            here += wy[d]
        wz[z] = here
        for d in range(1, nz):
            remote(wz.at[z], wz.at[z], st_send.at[5], st_recv.at[5], {Z: to_z(d)}).start()

    started = set()
    for what, *of in plan(half, groups, LAG, SENDS, BATCHES):
        if what == "first":
            for way in range(2):
                ring_copy(way, of[0], 0).start()
        elif what == "acts":
            for i in of[0]:
                if i == far:
                    send_acts(to_z(half), far, 1, a2a_send.at[1], a2a_recv.at[far])
                else:
                    send_acts(to_z(i + 1), i, 0, a2a_send.at[0], a2a_recv.at[i])
                    send_acts(to_z(nz - 1 - i), i, 1, a2a_send.at[0], a2a_recv.at[i])
        elif what == "weights":
            weights_over_y()
        elif what == "hop":
            g, h = of
            for way in range(2):
                if h <= last_hop(way, g):
                    wait_bytes(G.at[g, 0, 0], ring_recv.at[way, g, h - 1])
                if h < last_hop(way, g):
                    ring_copy(way, g, h).start()
        elif what == "pairs":
            pairs_stage(*of)
        elif what == "dot":
            g, todo = of
            for i in todo:
                product = lax.dot_general(
                    G[g, i].reshape(2 * tok, LANE), A[i].reshape(2 * tok, rows_z),
                    (((0,), (0,)), ((), ())), preferred_element_type=jnp.float32,
                )
                for yy in range(ny):
                    block = product[:, yy * LANE:(yy + 1) * LANE]
                    part[g, yy] = part[g, yy] + block if g in started else block
                started.add(g)
        elif what == "scatter":
            g = of[0]
            for d in ys:
                there = lax.rem(y + d, ny)
                remote(part.at[g, there], R.at[g, d - 1], y_send.at[0], y_recv.at[g], {Y: there}).start()

    weights_over_z()

    row_sq = jnp.zeros((1, LANE), jnp.float32)
    for g in range(groups):
        if g == groups - 1:
            wait_bytes(A.at[pl.ds(0, half - 1), :, pl.ds(0, share), :], a2a_send.at[0])
            wait_bytes(A.at[0, 0, pl.ds(0, share), :], a2a_send.at[1])
            wait_bytes(A.at[pl.ds(0, half - 1), :, pl.ds(0, share * (nx - 1)), :], x_send.at[0])
            wait_bytes(A.at[0, 0, pl.ds(0, share * (nx - 1)), :], x_send.at[1])
            wait_bytes(A.at[pl.ds(0, half - 1), :, pl.ds(0, core_rows), :], d_send.at[0])
            wait_bytes(A.at[0, 0, pl.ds(0, core_rows), :], d_send.at[1])
            for way in range(2):
                wait_bytes(G.at[0], ring_send.at[way, 0])
                wait_bytes(G.at[0, pl.ds(0, half - 1)], ring_send.at[way, 1])
            wait_bytes(wy.at[pl.ds(0, ny - 1)], st_send.at[4])
        wait_bytes(R.at[0], y_recv.at[g])
        total = part[g, y]
        for d in range(ny - 1):
            total += R[g, d]
        row_sq += jnp.sum(total * total + floor_eps, axis=0, keepdims=True)
        if g < groups - 1:
            grad[:, g * LANE:(g + 1) * LANE] = total.T

    st1[xc] = jnp.broadcast_to(row_sq, (8, LANE))
    for k in peers:
        remote(st1.at[xc], st1.at[xc], st_send.at[0], st_recv.at[0], col_peer(k)).start()
    grad[:, (groups - 1) * LANE:] = total.T
    for g in range(groups):
        grads = grad[:, g * LANE:(g + 1) * LANE]
        st2[y, g:g + 1, :] = jnp.sum(grads * grads + floor_eps, axis=0, keepdims=True)
    wait_bytes(part.at[:, pl.ds(0, ny - 1)], y_send.at[0])
    wait_bytes(st1.at[pl.ds(0, nx * nc - 1)], st_send.at[0])

    wait_bytes(st1.at[pl.ds(0, nx * nc - 1)], st_recv.at[0])
    row_total = st1[0, 0:1, :]
    for k in range(1, nx * nc):
        row_total += st1[k, 0:1, :]
    row_moment = decay_rate * rs_v[...] + (1.0 - decay_rate) * (row_total / cols_all)
    inverse = jnp.broadcast_to(1.0 / row_moment, (LANE, LANE)).T
    for g in range(groups):
        grads = grad[:, g * LANE:(g + 1) * LANE]
        st2[y, 4 + g:5 + g, :] = jnp.sum(grads * grads * inverse, axis=0, keepdims=True)

    for d in ys:
        remote(st2.at[y], st2.at[y], st_send.at[1], st_recv.at[1], {Y: lax.rem(y + d, ny)}).start()
    row_out[...] = row_moment
    rows_down = jnp.broadcast_to(row_moment, (LANE, LANE)).T
    wait_bytes(st2.at[pl.ds(0, ny - 1)], st_send.at[1])
    wait_bytes(st2.at[pl.ds(0, ny - 1)], st_recv.at[1])
    over_y = st2[0]
    for d in range(1, ny):
        over_y += st2[d]
    st3[z] = over_y
    for d in zs:
        remote(st3.at[z], st3.at[z], st_send.at[2], st_recv.at[2], {Z: to_z(d)}).start()
    wait_bytes(wz.at[pl.ds(0, nz - 1)], st_send.at[5])
    wait_bytes(wz.at[pl.ds(0, nz - 1)], st_recv.at[5])
    weight_total = wz[0]
    for d in range(1, nz):
        weight_total += wz[d]
    st4[xc, 4:8, :] = jnp.broadcast_to(weight_total, (4, LANE))
    wait_bytes(st3.at[pl.ds(0, nz - 1)], st_send.at[2])
    wait_bytes(st3.at[pl.ds(0, nz - 1)], st_recv.at[2])
    over_z = st3[0]
    for d in range(1, nz):
        over_z += st3[d]
    col_moment = decay_rate * cs_v[...] + (1.0 - decay_rate) * (over_z[0:groups] / width)
    st4[xc, 0:4, :] = over_z[4:4 + groups] / col_moment

    for k in peers:
        remote(st4.at[xc], st4.at[xc], st_send.at[3], st_recv.at[3], col_peer(k)).start()
    col_out[...] = col_moment
    for g in range(groups):
        lanes = slice(g * LANE, (g + 1) * LANE)
        grad[:, lanes] = grad[:, lanes] * lax.rsqrt(rows_down * col_moment[g:g + 1, :])
    leaving = pltpu.make_async_copy(grad, unclipped_out, local_sem.at[0])
    leaving.start()
    wait_bytes(st4.at[pl.ds(0, nx * nc - 1)], st_recv.at[3])
    over_x = st4[0]
    for k in range(1, nx * nc):
        over_x += st4[k]
    update_total = jnp.sum(over_x[0:4], keepdims=True)
    weight_total = jnp.sum(over_x[4:5], keepdims=True)
    clip_out[...] = jnp.broadcast_to(jnp.maximum(1.0, jnp.sqrt(update_total / count_all)), clip_out.shape)
    step_out[...] = jnp.broadcast_to(relative_rate * jnp.sqrt(weight_total / count_all + 1e-06), step_out.shape)
    wait_bytes(st4.at[pl.ds(0, nx * nc - 1)], st_send.at[3])
    leaving.wait()


def finish(unclipped, weight, row_moment, col_moment, clip_factor, step_size, new_weight, update, row_out, col_out):
    row_out[...] = row_moment[...]
    col_out[...] = col_moment[...]
    for g in range(col_moment.shape[0]):
        lanes = slice(g * LANE, (g + 1) * LANE)
        clipped = unclipped[:, lanes] / clip_factor[g:g + 1, :]
        update[:, lanes] = clipped
        new_weight[:, lanes] = weight[:, lanes] - step_size[g:g + 1, :] * clipped


def per_device(acts, out_grads, weight, row_state, col_state):
    nz, ny, nx, nc = (lax.axis_size(a) for a in (Z, Y, X, C))
    tok, width = acts.shape
    cols = out_grads.shape[1]
    groups = cols // LANE
    half = nz // 2
    rows_z = ny * LANE
    anywhere = pl.BlockSpec(memory_space=pl.ANY)
    vmem = pl.BlockSpec(memory_space=pltpu.VMEM)
    f32 = jnp.float32
    unclipped, row_moment, col_moment, clip_factor, step_size = pl.pallas_call(
        functools.partial(kernel, (nz, ny, nx, nc, tok, cols, width)),
        out_shape=(
            jax.ShapeDtypeStruct((LANE, cols), f32),
            jax.ShapeDtypeStruct((1, LANE), f32),
            jax.ShapeDtypeStruct((groups, LANE), f32),
            jax.ShapeDtypeStruct((groups, LANE), f32),
            jax.ShapeDtypeStruct((groups, LANE), f32),
        ),
        in_specs=[anywhere] * 5,
        out_specs=[anywhere] + [vmem] * 4,
        scratch_shapes=[
            pltpu.VMEM((half, 2, tok, rows_z), jnp.bfloat16),
            pltpu.VMEM((groups, half, 2, tok, LANE), jnp.bfloat16),
            pltpu.VMEM((groups, ny, LANE, LANE), f32),
            pltpu.VMEM((groups, ny - 1, LANE, LANE), f32),
            pltpu.VMEM((LANE, cols), f32),
            pltpu.VMEM((LANE, cols), f32),
            pltpu.VMEM((1, LANE), f32),
            pltpu.VMEM((groups, LANE), f32),
            pltpu.VMEM((nx * nc, 8, LANE), f32),
            pltpu.VMEM((ny, 8, LANE), f32),
            pltpu.VMEM((nz, 8, LANE), f32),
            pltpu.VMEM((nx * nc, 8, LANE), f32),
            pltpu.VMEM((ny, 1, LANE), f32),
            pltpu.VMEM((nz, 1, LANE), f32),
            pltpu.SemaphoreType.DMA((groups + 4,)),
            pltpu.SemaphoreType.DMA((2,)),
            pltpu.SemaphoreType.DMA((half,)),
            pltpu.SemaphoreType.DMA((2,)),
            pltpu.SemaphoreType.DMA((half,)),
            pltpu.SemaphoreType.DMA((2,)),
            pltpu.SemaphoreType.DMA((half,)),
            pltpu.SemaphoreType.DMA((2, 2)),
            pltpu.SemaphoreType.DMA((2, groups, half)),
            pltpu.SemaphoreType.DMA((1,)),
            pltpu.SemaphoreType.DMA((groups,)),
            pltpu.SemaphoreType.DMA((6,)),
            pltpu.SemaphoreType.DMA((6,)),
        ],
        compiler_params=pltpu.CompilerParams(
            collective_id=0, has_side_effects=True, vmem_limit_bytes=60 * 1024 * 1024
        ),
    )(acts, out_grads, weight, row_state.reshape(1, LANE), col_state.reshape(groups, LANE))
    new_weight, update, row_moment, col_moment = pl.pallas_call(
        finish,
        out_shape=(
            jax.ShapeDtypeStruct((LANE, cols), f32),
            jax.ShapeDtypeStruct((LANE, cols), f32),
            jax.ShapeDtypeStruct((1, LANE), f32),
            jax.ShapeDtypeStruct((groups, LANE), f32),
        ),
        in_specs=[vmem] * 6,
        out_specs=[vmem] * 4,
    )(unclipped, weight, row_moment, col_moment, clip_factor, step_size)
    return (new_weight, update, row_moment.reshape(-1), col_moment.reshape(-1))


def solution(mesh):
    finer = Mesh(mesh.devices.reshape(16, 4, 4, 2), (Z, Y, X, C))
    return jax.shard_map(
        per_device,
        mesh=finer,
        in_specs=(P(ROW, None), P(ROW, COL), P(ROW, COL), P(ROW), P(COL)),
        out_specs=(P(ROW, COL), P(ROW, COL), P(ROW), P(COL)),
        check_vma=False,
    )
```

```python
import functools

import jax
import jax.numpy as jnp
from jax import lax
from jax.experimental import pallas as pl
from jax.experimental.pallas import tpu as pltpu
from jax.sharding import Mesh
from jax.sharding import PartitionSpec as P

Z, Y, X, C = "z", "y", "x", "c"
ROW = (Z, Y)
COL = (X, C)
LANE = 128
LAG = (0, 0, 1, 2)
SENDS = (([7], 0), ([6], 1), ([5], 1), ([4], 2), ([3], 2), ([2], 2), ([1], 3), ([0], 3))
BATCHES = (([7], 2), ([5, 6], 3), ([2, 3, 4], 4), ([0, 1], 5))

decay_rate = 0.85
floor_eps = 1e-30
relative_rate = 0.05


def plan(half, groups, lag, sends, batches):
    steps = [("first", g) for g in range(groups) if lag[g] == 0]
    steps += [("acts", pairs) for pairs, at in sends if at == 0]
    steps.append(("weights",))
    steps += [("first", g) for g in range(groups) if lag[g] == 1]
    ready, done = [], {g: [] for g in range(groups)}
    arrived = {g: [] for g in range(groups)}

    def multiply(g):
        todo = [i for i in arrived[g] if i in ready and i not in done[g]]
        done[g] += todo
        if todo:
            steps.append(("dot", g, todo))
        if len(done[g]) == half:
            steps.append(("scatter", g))

    for r in range(1, half + max(lag) + 1):
        for g in range(groups):
            if lag[g] == r and r > 1:
                steps.append(("first", g))
            h = r - lag[g]
            if 1 <= h <= half:
                steps.append(("hop", g, h))
                arrived[g].append(h - 1)
                if h == half and len(ready) == half:
                    multiply(g)
        steps += [("acts", pairs) for pairs, at in sends if at == r]
        for stage in (1, 2, 3):
            for pairs, at in batches:
                if at + stage - 1 == r:
                    steps.append(("pairs", stage, pairs))
                    if stage == 3:
                        ready += pairs
        for g in range(groups):
            if len(done[g]) < half:
                multiply(g)
    assert all(len(done[g]) == half for g in range(groups))
    return steps


def kernel(
    sizes,
    acts, og, weight, row_state, col_state,
    unclipped_out, row_out, col_out, clip_out, step_out,
    A, G, part, R, grad, wv, rs_v, cs_v, st1, st2, st3, st4, wy, wz,
    local_sem, a2a_send, a2a_recv, x_send, x_recv, d_send, d_recv,
    ring_send, ring_recv, y_send, y_recv, st_send, st_recv,
):
    nz, ny, nx, nc, tok, cols, width = sizes
    half = nz // 2
    groups = cols // LANE
    rows_z = ny * LANE
    share = tok // (nx * nc)
    core_rows = share * nx
    cols_all = cols * nx * nc
    count_all = width * cols_all
    z, y, x, c = (lax.axis_index(a) for a in (Z, Y, X, C))
    xc = x * nc + c
    own = c * core_rows + x * share
    far = half - 1

    def to_z(d):
        return lax.rem(z + d, nz)

    def remote(src, dst, send, recv, where):
        return pltpu.make_async_remote_copy(
            src_ref=src, dst_ref=dst, send_sem=send, recv_sem=recv,
            device_id=where, device_id_type=pl.DeviceIdType.MESH,
        )

    def wait_bytes(ref, sem):
        pltpu.make_async_copy(ref, ref, sem).wait()

    ys = sorted(range(1, ny), key=lambda d: -min(d, ny - d))
    xs = sorted(range(1, nx), key=lambda d: -min(d, nx - d))
    zs = sorted(range(1, nz), key=lambda d: -min(d, nz - d))
    peers = [(d, e) for d in xs for e in range(nc)] + [(0, e) for e in range(1, nc)]

    def col_peer(k):
        d, e = k
        return {X: lax.rem(x + d, nx), C: lax.rem(c + e, nc)}

    own_cols = pl.ds(pl.multiple_of(z * rows_z, LANE), rows_z)
    local = [
        pltpu.make_async_copy(og.at[:, pl.ds(g * LANE, LANE)], G.at[g, far, 0], local_sem.at[g])
        for g in range(groups)
    ] + [
        pltpu.make_async_copy(acts.at[:, own_cols], A.at[far, 0], local_sem.at[groups]),
        pltpu.make_async_copy(weight, wv, local_sem.at[groups + 1]),
        pltpu.make_async_copy(row_state, rs_v, local_sem.at[groups + 2]),
        pltpu.make_async_copy(col_state, cs_v, local_sem.at[groups + 3]),
    ]

    barrier = pltpu.get_barrier_semaphore()
    for d in zs:
        pl.semaphore_signal(barrier, inc=1, device_id={Z: to_z(d)}, device_id_type=pl.DeviceIdType.MESH)
    for d in range(1, ny):
        pl.semaphore_signal(barrier, inc=1, device_id={Y: lax.rem(y + d, ny)}, device_id_type=pl.DeviceIdType.MESH)
    for k in peers:
        pl.semaphore_signal(barrier, inc=1, device_id=col_peer(k), device_id_type=pl.DeviceIdType.MESH)
    for copy in local:
        copy.start()
    for copy in local:
        copy.wait()
    weight_sq = jnp.sum(wv[...] * wv[...], axis=0, keepdims=True)
    weight_sq = sum(weight_sq[:, g * LANE:(g + 1) * LANE] for g in range(groups))
    wy[y] = weight_sq
    pl.semaphore_wait(barrier, nz - 1 + ny - 1 + nx * nc - 1)

    own_rows = pl.ds(pl.multiple_of(own, share), share)
    core_part = pl.ds(pl.multiple_of(c * core_rows, core_rows), core_rows)
    sibling = {C: nc - 1 - c}

    def send_acts(target, i, q, send, recv):
        there = pl.ds(pl.multiple_of(target * rows_z, LANE), rows_z)
        remote(acts.at[own_rows, there], A.at[i, q, own_rows, :], send, recv, {Z: target}).start()

    def last_hop(way, g):
        return half if (g % 2 == 0) == (way == 0) else half - 1

    def ring_copy(way, g, h):
        src = G.at[g, h - 1, way] if h else G.at[g, far, 0]
        q = 1 if h + 1 == half else way
        return remote(
            src, G.at[g, h, q], ring_send.at[way, 0 if last_hop(way, g) == half else 1],
            ring_recv.at[way, g, h], {Z: to_z(1 if way == 0 else nz - 1)},
        )

    def pairs_stage(stage, pairs):
        i, n = pairs[0], len(pairs)
        if pairs == [far]:
            block, kind = (lambda rows: A.at[far, 1, rows, :]), 1
        else:
            block, kind = (lambda rows: A.at[pl.ds(i, n), :, rows, :]), 0
        if stage == 1:
            for j in pairs:
                wait_bytes(A.at[far, 1, pl.ds(0, share), :] if kind else A.at[0, :, pl.ds(0, share), :], a2a_recv.at[j])
            for d in xs:
                remote(block(own_rows), block(own_rows), x_send.at[kind], x_recv.at[i], {X: lax.rem(x + d, nx)}).start()
        elif stage == 2:
            wait_bytes(block(pl.ds(0, share * (nx - 1))), x_recv.at[i])
            remote(block(core_part), block(core_part), d_send.at[kind], d_recv.at[i], sibling).start()
        else:
            wait_bytes(block(pl.ds(0, core_rows)), d_recv.at[i])

    def weights_over_y():
        for d in range(1, ny):
            remote(wy.at[y], wy.at[y], st_send.at[4], st_recv.at[4], {Y: lax.rem(y + d, ny)}).start()

    def weights_over_z():
        wait_bytes(wy.at[pl.ds(0, ny - 1)], st_recv.at[4])
        here = wy[0]
        for d in range(1, ny):
            here += wy[d]
        wz[z] = here
        for d in range(1, nz):
            remote(wz.at[z], wz.at[z], st_send.at[5], st_recv.at[5], {Z: to_z(d)}).start()

    started = set()
    for what, *of in plan(half, groups, LAG, SENDS, BATCHES):
        if what == "first":
            for way in range(2):
                ring_copy(way, of[0], 0).start()
        elif what == "acts":
            for i in of[0]:
                if i == far:
                    send_acts(to_z(half), far, 1, a2a_send.at[1], a2a_recv.at[far])
                else:
                    send_acts(to_z(i + 1), i, 0, a2a_send.at[0], a2a_recv.at[i])
                    send_acts(to_z(nz - 1 - i), i, 1, a2a_send.at[0], a2a_recv.at[i])
        elif what == "weights":
            weights_over_y()
        elif what == "hop":
            g, h = of
            for way in range(2):
                if h <= last_hop(way, g):
                    wait_bytes(G.at[g, 0, 0], ring_recv.at[way, g, h - 1])
                if h < last_hop(way, g):
                    ring_copy(way, g, h).start()
        elif what == "pairs":
            pairs_stage(*of)
        elif what == "dot":
            g, todo = of
            for i in todo:
                product = lax.dot_general(
                    G[g, i].reshape(2 * tok, LANE), A[i].reshape(2 * tok, rows_z),
                    (((0,), (0,)), ((), ())), preferred_element_type=jnp.float32,
                )
                for yy in range(ny):
                    block = product[:, yy * LANE:(yy + 1) * LANE]
                    part[g, yy] = part[g, yy] + block if g in started else block
                started.add(g)
        elif what == "scatter":
            g = of[0]
            for d in ys:
                there = lax.rem(y + d, ny)
                remote(part.at[g, there], R.at[g, d - 1], y_send.at[0], y_recv.at[g], {Y: there}).start()

    row_sq = jnp.zeros((1, LANE), jnp.float32)
    for g in range(groups):
        if g == groups - 1:
            wait_bytes(A.at[pl.ds(0, half - 1), :, pl.ds(0, share), :], a2a_send.at[0])
            wait_bytes(A.at[0, 0, pl.ds(0, share), :], a2a_send.at[1])
            wait_bytes(A.at[pl.ds(0, half - 1), :, pl.ds(0, share * (nx - 1)), :], x_send.at[0])
            wait_bytes(A.at[0, 0, pl.ds(0, share * (nx - 1)), :], x_send.at[1])
            wait_bytes(A.at[pl.ds(0, half - 1), :, pl.ds(0, core_rows), :], d_send.at[0])
            wait_bytes(A.at[0, 0, pl.ds(0, core_rows), :], d_send.at[1])
            for way in range(2):
                wait_bytes(G.at[0], ring_send.at[way, 0])
                wait_bytes(G.at[0, pl.ds(0, half - 1)], ring_send.at[way, 1])
        wait_bytes(R.at[0], y_recv.at[g])
        total = part[g, y]
        for d in range(ny - 1):
            total += R[g, d]
        row_sq += jnp.sum(total * total + floor_eps, axis=0, keepdims=True)
        if g < groups - 1:
            grad[:, g * LANE:(g + 1) * LANE] = total.T

    st1[xc] = row_sq
    for k in peers:
        remote(st1.at[xc], st1.at[xc], st_send.at[0], st_recv.at[0], col_peer(k)).start()
    grad[:, (groups - 1) * LANE:] = total.T
    for g in range(groups):
        grads = grad[:, g * LANE:(g + 1) * LANE]
        st2[y, g:g + 1, :] = jnp.sum(grads * grads + floor_eps, axis=0, keepdims=True)
    weights_over_z()
    wait_bytes(wy.at[pl.ds(0, ny - 1)], st_send.at[4])
    wait_bytes(part.at[:, pl.ds(0, ny - 1)], y_send.at[0])
    wait_bytes(st1.at[pl.ds(0, nx * nc - 1)], st_send.at[0])

    wait_bytes(st1.at[pl.ds(0, nx * nc - 1)], st_recv.at[0])
    row_total = st1[0]
    for k in range(1, nx * nc):
        row_total += st1[k]
    row_moment = decay_rate * rs_v[...] + (1.0 - decay_rate) * (row_total / cols_all)
    inverse = jnp.broadcast_to(1.0 / row_moment, (LANE, LANE)).T
    for g in range(groups):
        grads = grad[:, g * LANE:(g + 1) * LANE]
        st2[y, 4 + g:5 + g, :] = jnp.sum(grads * grads * inverse, axis=0, keepdims=True)

    for d in ys:
        remote(st2.at[y], st2.at[y], st_send.at[1], st_recv.at[1], {Y: lax.rem(y + d, ny)}).start()
    row_out[...] = row_moment
    rows_down = jnp.broadcast_to(row_moment, (LANE, LANE)).T
    wait_bytes(st2.at[pl.ds(0, ny - 1)], st_send.at[1])
    wait_bytes(st2.at[pl.ds(0, ny - 1)], st_recv.at[1])
    over_y = st2[0]
    for d in range(1, ny):
        over_y += st2[d]
    st3[z] = over_y
    for d in zs:
        remote(st3.at[z], st3.at[z], st_send.at[2], st_recv.at[2], {Z: to_z(d)}).start()
    wait_bytes(wz.at[pl.ds(0, nz - 1)], st_send.at[5])
    wait_bytes(wz.at[pl.ds(0, nz - 1)], st_recv.at[5])
    weight_total = wz[0]
    for d in range(1, nz):
        weight_total += wz[d]
    st4[xc, 4:8, :] = jnp.broadcast_to(weight_total, (4, LANE))
    wait_bytes(st3.at[pl.ds(0, nz - 1)], st_send.at[2])
    wait_bytes(st3.at[pl.ds(0, nz - 1)], st_recv.at[2])
    over_z = st3[0]
    for d in range(1, nz):
        over_z += st3[d]
    col_moment = decay_rate * cs_v[...] + (1.0 - decay_rate) * (over_z[0:groups] / width)
    st4[xc, 0:4, :] = over_z[4:4 + groups] / col_moment

    for k in peers:
        remote(st4.at[xc], st4.at[xc], st_send.at[3], st_recv.at[3], col_peer(k)).start()
    col_out[...] = col_moment
    for g in range(groups):
        lanes = slice(g * LANE, (g + 1) * LANE)
        grad[:, lanes] = grad[:, lanes] * lax.rsqrt(rows_down * col_moment[g:g + 1, :])
    leaving = pltpu.make_async_copy(grad, unclipped_out, local_sem.at[0])
    leaving.start()
    wait_bytes(st4.at[pl.ds(0, nx * nc - 1)], st_recv.at[3])
    over_x = st4[0]
    for k in range(1, nx * nc):
        over_x += st4[k]
    update_total = jnp.sum(over_x[0:4], keepdims=True)
    weight_total = jnp.sum(over_x[4:5], keepdims=True)
    clip_out[...] = jnp.broadcast_to(jnp.maximum(1.0, jnp.sqrt(update_total / count_all)), clip_out.shape)
    step_out[...] = jnp.broadcast_to(relative_rate * jnp.sqrt(weight_total / count_all + 1e-06), step_out.shape)
    wait_bytes(st4.at[pl.ds(0, nx * nc - 1)], st_send.at[3])
    leaving.wait()


def finish(unclipped, weight, row_moment, col_moment, clip_factor, step_size, new_weight, update, row_out, col_out):
    row_out[...] = row_moment[...]
    col_out[...] = col_moment[...]
    for g in range(col_moment.shape[0]):
        lanes = slice(g * LANE, (g + 1) * LANE)
        clipped = unclipped[:, lanes] / clip_factor[g:g + 1, :]
        update[:, lanes] = clipped
        new_weight[:, lanes] = weight[:, lanes] - step_size[g:g + 1, :] * clipped


def per_device(acts, out_grads, weight, row_state, col_state):
    nz, ny, nx, nc = (lax.axis_size(a) for a in (Z, Y, X, C))
    tok, width = acts.shape
    cols = out_grads.shape[1]
    groups = cols // LANE
    half = nz // 2
    rows_z = ny * LANE
    anywhere = pl.BlockSpec(memory_space=pl.ANY)
    vmem = pl.BlockSpec(memory_space=pltpu.VMEM)
    f32 = jnp.float32
    unclipped, row_moment, col_moment, clip_factor, step_size = pl.pallas_call(
        functools.partial(kernel, (nz, ny, nx, nc, tok, cols, width)),
        out_shape=(
            jax.ShapeDtypeStruct((LANE, cols), f32),
            jax.ShapeDtypeStruct((1, LANE), f32),
            jax.ShapeDtypeStruct((groups, LANE), f32),
            jax.ShapeDtypeStruct((groups, LANE), f32),
            jax.ShapeDtypeStruct((groups, LANE), f32),
        ),
        in_specs=[anywhere] * 5,
        out_specs=[anywhere] + [vmem] * 4,
        scratch_shapes=[
            pltpu.VMEM((half, 2, tok, rows_z), jnp.bfloat16),
            pltpu.VMEM((groups, half, 2, tok, LANE), jnp.bfloat16),
            pltpu.VMEM((groups, ny, LANE, LANE), f32),
            pltpu.VMEM((groups, ny - 1, LANE, LANE), f32),
            pltpu.VMEM((LANE, cols), f32),
            pltpu.VMEM((LANE, cols), f32),
            pltpu.VMEM((1, LANE), f32),
            pltpu.VMEM((groups, LANE), f32),
            pltpu.VMEM((nx * nc, 1, LANE), f32),
            pltpu.VMEM((ny, 8, LANE), f32),
            pltpu.VMEM((nz, 8, LANE), f32),
            pltpu.VMEM((nx * nc, 8, LANE), f32),
            pltpu.VMEM((ny, 1, LANE), f32),
            pltpu.VMEM((nz, 1, LANE), f32),
            pltpu.SemaphoreType.DMA((groups + 4,)),
            pltpu.SemaphoreType.DMA((2,)),
            pltpu.SemaphoreType.DMA((half,)),
            pltpu.SemaphoreType.DMA((2,)),
            pltpu.SemaphoreType.DMA((half,)),
            pltpu.SemaphoreType.DMA((2,)),
            pltpu.SemaphoreType.DMA((half,)),
            pltpu.SemaphoreType.DMA((2, 2)),
            pltpu.SemaphoreType.DMA((2, groups, half)),
            pltpu.SemaphoreType.DMA((1,)),
            pltpu.SemaphoreType.DMA((groups,)),
            pltpu.SemaphoreType.DMA((6,)),
            pltpu.SemaphoreType.DMA((6,)),
        ],
        compiler_params=pltpu.CompilerParams(
            collective_id=0, has_side_effects=True, vmem_limit_bytes=60 * 1024 * 1024
        ),
    )(acts, out_grads, weight, row_state.reshape(1, LANE), col_state.reshape(groups, LANE))
    new_weight, update, row_moment, col_moment = pl.pallas_call(
        finish,
        out_shape=(
            jax.ShapeDtypeStruct((LANE, cols), f32),
            jax.ShapeDtypeStruct((LANE, cols), f32),
            jax.ShapeDtypeStruct((1, LANE), f32),
            jax.ShapeDtypeStruct((groups, LANE), f32),
        ),
        in_specs=[vmem] * 6,
        out_specs=[vmem] * 4,
    )(unclipped, weight, row_moment, col_moment, clip_factor, step_size)
    return (new_weight, update, row_moment.reshape(-1), col_moment.reshape(-1))


def solution(mesh):
    finer = Mesh(mesh.devices.reshape(16, 4, 4, 2), (Z, Y, X, C))
    return jax.shard_map(
        per_device,
        mesh=finer,
        in_specs=(P(ROW, None), P(ROW, COL), P(ROW, COL), P(ROW), P(COL)),
        out_specs=(P(ROW, COL), P(ROW, COL), P(ROW), P(COL)),
        check_vma=False,
    )
```
